256 devices in a mesh: seq: 32 (over x, z_lo, core), head: 8 (over y, z_hi).
Axes of the slice: x: 4, y: 4, z: 8 (z_hi: 2, z_lo: 4; z = z_hi * 4 + z_lo), core: 2. Of those that a mesh axis runs over, the one named last changes fastest.
Arguments:
- query_states: bfloat16 [8192, 8192], P(('seq', 'head')), may hold values from -8 to 8
- key_states: bfloat16 [8192, 1024], P(('seq', 'head')), may hold values from -8 to 8
- value_states: bfloat16 [8192, 1024], P(('seq', 'head')), may hold values from -6 to 6
- seg_ids: int32 [8192], P('seq'), may hold values from 0 to 9, as said below
- seg_starts: int32 [10], replicated, may hold values from 0 to 7168, as said below
Outputs:
- attended: bfloat16 [8192, 8192], P(('seq', 'head'))
The draws below stay inside these ranges and needn't reach their ends.
Inputs may be any that keep to these rules, and one draw needn't show every extreme that they name: `seg_ids`: 0 on a prompt at the start, 1 to 8 on the eight responses in order, 9 on a summary at the end; never falling; the prompt holds 512 to 1024 positions, the summary exactly 1024. `seg_starts`: entry 0 is 0, entries rise strictly, entry 9 is 7168.
All inputs are finite; a program needn't handle non-finite values.
Results may differ from the reference program's by a relative error of at most 0.0045.
Values may be sent and summed in bfloat16 or wider, within the bound.
A program may use at most 64 MiB of HBM per device.

```python
import math
import jax
import jax.numpy as jnp
from jax import lax

HQ = 64
KV_HEADS = 8
HD = 128
CTX = 8192
QW = 8192
KW = 1024


def segment_layout(key):
    shared = jax.random.fold_in(key, 7)
    first_key = jax.random.fold_in(shared, 0)
    third_key = jax.random.fold_in(shared, 2)
    prompt_len = jax.random.randint(first_key, (), CTX // 16, CTX // 8 + 1).astype(jnp.int32)
    summary_len = jnp.int32(CTX // 8)
    shares_raw = jax.random.randint(third_key, (8,), 1, 9).astype(jnp.int32)
    remaining = CTX - prompt_len - summary_len
    shares = remaining * shares_raw // jnp.sum(shares_raw)
    shares = shares.at[7].add(remaining - jnp.sum(shares))
    running = jnp.concatenate([jnp.zeros((1,), jnp.int32), jnp.cumsum(shares).astype(jnp.int32)])
    starts = jnp.concatenate([jnp.zeros((1,), jnp.int32), prompt_len + running])
    return starts.astype(jnp.int32)


def draw_seg_starts(key, part):
    return segment_layout(key)


def draw_seg_ids(key, part):
    starts = segment_layout(key)
    positions = jnp.arange(CTX, dtype=jnp.int32)
    passed = (positions[:, None] >= starts[None, 1:]).astype(jnp.int32)
    return jnp.sum(passed, axis=1).astype(jnp.int32)


def draw_query_states(key, part):
    base = jnp.clip(jax.random.normal(jax.random.fold_in(key, 3), (CTX, QW), jnp.float32), -6.0, 6.0)
    return base.astype(jnp.bfloat16)


def draw_key_states(key, part):
    base = jnp.clip(jax.random.normal(jax.random.fold_in(key, 5), (CTX, KW), jnp.float32), -6.0, 6.0)
    return base.astype(jnp.bfloat16)


def steps_of(own_key, shape, cuts, smallest, largest):
    loudness, own = 1.0, jax.random.fold_in(own_key, 6)
    for axis_at, blocks in cuts:
        steps = jnp.exp(jax.random.uniform(jax.random.fold_in(own, axis_at), (blocks,), jnp.float32, smallest / len(cuts), largest / len(cuts)))
        loudness = loudness * jnp.repeat(steps, shape[axis_at] // blocks).reshape([-1 if axis == axis_at else 1 for axis in range(len(shape))])
    return loudness


def centred(rng, shape, deviation, bound, shards=(), kind=jnp.bfloat16):
    drawn = deviation * jax.random.normal(rng, shape, jnp.float32)
    if shards:
        drawn = drawn * steps_of(rng, shape, shards, -0.22, 0.18)
    return jnp.clip(drawn, -bound, bound).astype(kind)


def setup_inputs(seed: int = 0) -> dict:
    arg_keys = jax.random.split(jax.random.key(seed), 6)
    query_states = draw_query_states(jax.random.fold_in(arg_keys[5], 71), 0)
    key_states = draw_key_states(jax.random.fold_in(arg_keys[5], 71), 0)
    value_states = centred(arg_keys[2], (CTX, KW), 1.0, 6.0, ((0, 256),))
    seg_ids = draw_seg_ids(jax.random.fold_in(arg_keys[5], 71), 0)
    seg_starts = draw_seg_starts(jax.random.fold_in(arg_keys[5], 71), 0)
    return {"query_states": query_states, "key_states": key_states, "value_states": value_states, "seg_ids": seg_ids, "seg_starts": seg_starts}


def visible_keys(query_pos, query_seg, own_start, key_pos, first_response):
    causal = key_pos[None, :] <= query_pos[:, None]
    allowed = (key_pos[None, :] < first_response) | (key_pos[None, :] >= own_start[:, None]) | (query_seg[:, None] == 9)
    return causal & allowed

def segment_start(seg_rows, seg_starts):
    labels = jnp.arange(10, dtype=jnp.int32)
    picked = jnp.where(seg_rows[:, None] == labels[None, :], seg_starts[None, :], 0)
    return lax.optimization_barrier(jnp.sum(picked, axis=1)).astype(jnp.int32)

def reference(query_states, key_states, value_states, seg_ids, seg_starts):
    score_scale = 1.0 / math.sqrt(HD)
    key_pos = jnp.arange(CTX, dtype=jnp.int32)
    own_start = segment_start(seg_ids, seg_starts)
    first_response = seg_starts[1]
    block_rows = math.gcd(512, CTX)
    head_keys = jnp.moveaxis(key_states.reshape(CTX, KV_HEADS, HD), 1, 0)
    head_values = jnp.moveaxis(value_states.reshape(CTX, KV_HEADS, HD), 1, 0)

    def one_block(block_index):
        row_start = (block_index * block_rows).astype(jnp.int32)
        query_block = lax.dynamic_slice_in_dim(query_states, row_start, block_rows, 0)
        query_block = query_block.reshape(block_rows, KV_HEADS, HQ // KV_HEADS, HD)
        query_pos = row_start + jnp.arange(block_rows, dtype=jnp.int32)
        seg_block = lax.dynamic_slice_in_dim(seg_ids, row_start, block_rows, 0)
        start_block = lax.dynamic_slice_in_dim(own_start, row_start, block_rows, 0)
        visible = visible_keys(query_pos, seg_block, start_block, key_pos, first_response)

        def per_head(operands):
            query_head, key_head, value_head = operands
            scores = jnp.einsum('bgd,kd->bgk', query_head.astype(jnp.float32), key_head.astype(jnp.float32)) * score_scale
            scores = jnp.where(visible[:, None, :], scores, -jnp.inf)
            row_top = lax.optimization_barrier(jnp.max(scores, axis=2, keepdims=True))
            weights = jnp.exp(scores - row_top)
            totals = lax.optimization_barrier(jnp.sum(weights, axis=2))
            rounded = weights.astype(jnp.bfloat16)
            mixed_out = jnp.einsum('bgk,kd->bgd', rounded.astype(jnp.float32), value_head.astype(jnp.float32))
            return mixed_out / totals[:, :, None]
        heads_done = lax.map(per_head, (jnp.moveaxis(query_block, 1, 0), head_keys, head_values))
        return jnp.moveaxis(heads_done, 0, 1).reshape(block_rows, HQ * HD).astype(jnp.bfloat16)
    blocks = lax.map(one_block, jnp.arange(CTX // block_rows, dtype=jnp.int32))
    return blocks.reshape(CTX, HQ * HD)
```

```python
import functools
import math

import jax
import jax.numpy as jnp
from jax import lax
from jax.experimental import pallas as pl
from jax.experimental.pallas import tpu as pltpu
from jax.sharding import PartitionSpec as P

MESH = pl.DeviceIdType.MESH
HD = 128
CHUNK = 32
GROUP = 8
CTX = 8192
SUMMARY_AT = 7168
KEYS = 512
NEG = -1e30
RATE = math.log2(math.e) / math.sqrt(HD)


class Place:
    def __init__(self):
        s, h = lax.axis_index("seq"), lax.axis_index("head")
        self.x, self.zb, self.p, self.core = s // 8, s // 4 % 2, s // 2 % 2, s % 2
        self.y, self.zhi = h // 2, h % 2
        self.group = self.y * 2 + self.p
        self.zp = self.zhi * 2 + self.zb
        self.late = jnp.logical_and(self.x == 3, self.zb == 1)

    def device(self, x=None, y=None, zp=None, p=None, core=None):
        x = self.x if x is None else x
        y = self.y if y is None else y
        zp = self.zp if zp is None else zp
        p = self.p if p is None else p
        core = self.core if core is None else core
        return ((x * 4 + (zp % 2) * 2 + p) * 2 + core, y * 2 + zp // 2)

    def partner(self, group):
        return self.device(y=group // 2, p=group % 2)

    def summary_worker(self, group):
        return self.device(x=self.y, y=group // 2, zp=self.zhi * 2 + self.p, p=group % 2)

    def summary_owner(self):
        return self.device(x=3, y=self.x, zp=self.zhi * 2 + 1, p=self.zb)

    def own_summary(self):
        return jnp.logical_and(self.late, jnp.logical_and(self.y == 3, self.p == 1))


def xor_bits(value, i):
    out = 0
    for b in (4, 2, 1):
        bit = value // b % 2
        out = out + b * ((1 - bit) if i & b else bit)
    return out


def slot_of(group):
    return group % 2 * 4 + group // 2


def cols(group, width):
    return pl.ds(pl.multiple_of(group * width, width), width)


def spread_kernel(q_ref, k_ref, v_ref, qg_ref, kv_ref, qs, qr, ks, kr, zxs, zxr, ls):
    me = Place()
    barrier = pltpu.get_barrier_semaphore()

    def greet(device):
        pl.semaphore_signal(barrier, inc=1, device_id=device, device_id_type=MESH)

    ring = {
        "z+": me.device(zp=(me.zp + 1) % 4),
        "z-": me.device(zp=(me.zp + 3) % 4),
        "x+": me.device(x=(me.x + 1) % 4),
        "x-": me.device(x=(me.x + 3) % 4),
        "t": me.device(core=1 - me.core),
    }
    own_sum = me.own_summary()
    for i in range(1, 8):
        greet(me.partner(xor_bits(me.group, i)))
    for device in ring.values():
        greet(device)

    @pl.when(jnp.logical_not(own_sum))
    def _():
        greet(me.summary_owner())

    readers = jnp.where(me.late, jnp.where(own_sum, 7, 8), 0)
    pl.semaphore_wait(barrier, 12 + readers)

    def copy(src, dst, send, recv, device):
        return pltpu.make_async_remote_copy(
            src_ref=src, dst_ref=dst, send_sem=send, recv_sem=recv, device_id=device, device_id_type=MESH
        )

    def kv_at(t, group):
        return kv_ref.at[t, me.x * 2 + me.zb, group % 2, me.core, group // 2, me.zhi]

    first = []
    for i in range(8):
        group = xor_bits(me.group, i)
        for t, ref in enumerate((k_ref, v_ref)):
            src = ref.at[:, cols(group, HD)]
            if i == 0:
                c = pltpu.make_async_copy(src, kv_at(t, me.group), ls.at[t])
            else:
                c = copy(src, kv_at(t, me.group), ks.at[i, t], kr.at[i, t], me.partner(group))
            c.start()
            first.append((i, t, c))

    def q_copy(i, summary):
        group = xor_bits(me.group, i)
        src = q_ref.at[:, cols(group, GROUP * HD)]
        if summary:
            return src, copy(src, qg_ref.at[8], qs.at[i], qr.at[8], me.summary_worker(group))
        return src, copy(src, qg_ref.at[slot_of(me.group)], qs.at[i], qr.at[i], me.partner(group))

    own_q = q_ref.at[:, cols(me.group, GROUP * HD)]
    local_q = pltpu.make_async_copy(own_q, qg_ref.at[slot_of(me.group)], ls.at[2])

    @pl.when(jnp.logical_not(me.late))
    def _():
        local_q.start()
        for i in range(1, 8):
            q_copy(i, False)[1].start()

    @pl.when(me.late)
    def _():
        for i in range(8):
            src, c = q_copy(i, True)
            if i == 0:

                @pl.when(own_sum)
                def _():
                    pltpu.make_async_copy(src, qg_ref.at[8], ls.at[2]).start()

                @pl.when(jnp.logical_not(own_sum))
                def _():
                    c.start()
            else:
                c.start()

    for i, t, c in first:
        if i == 0:
            c.wait()
        else:
            group = xor_bits(me.group, i)
            src = k_ref.at[:, cols(group, HD)]
            copy(src, kv_at(t, group), ks.at[i, t], kr.at[i, t], me.partner(group)).wait_recv()

    keys = {}

    def number(kind, dx, dz, t):
        return keys.setdefault((kind, dx, dz, t), len(keys))

    def piece(dx, dz, t):
        x, zp = (me.x + dx) % 4, (me.zp + dz) % 4
        return kv_ref.at[t, x * 2 + zp % 2, :, me.core, :, zp // 2]

    def far_piece(dx, dz, t):
        x, zp = (me.x + dx) % 4, (me.zp + dz) % 4
        return kv_ref.at[t, x * 2 + zp % 2, :, 1 - me.core, :, zp // 2]

    shift = {"z+": (0, -1), "z-": (0, 1), "x+": (-1, 0), "x-": (1, 0), "t": (0, 0)}
    sent = []

    def send(dx, dz, t, *ways):
        for way in ways:
            rx, rz = (dx + shift[way][0]) % 4, (dz + shift[way][1]) % 4
            n = number(way[0], rx, rz, t)
            ref = piece(dx, dz, t)
            c = copy(ref, ref, zxs.at[n], zxr.at[n], ring[way])
            c.start()
            sent.append(c)

    def wait(kind, dx, dz, t):
        n = number(kind, dx, dz, t)
        ref = far_piece(dx, dz, t) if kind == "t" else piece(dx, dz, t)
        copy(ref, ref, zxs.at[n], zxr.at[n], ring["t"]).wait_recv()

    for t in (0, 1):
        send(0, 0, t, "z+", "z-")
    for t in (0, 1):
        send(0, 0, t, "x+", "x-", "t")
    for dz, t in ((3, 0), (1, 1)):
        wait("z", 0, dz, t)
        send(0, dz, t, "z-" if t else "z+", "x+", "x-", "t")
    for dz, t in ((3, 1), (1, 0)):
        wait("z", 0, dz, t)
        send(0, dz, t, "x+", "x-", "t")
    for dx, t in ((3, 0), (1, 1)):
        wait("x", dx, 0, t)
        send(dx, 0, t, "x-" if t else "x+", "t")
    for dz, t in ((2, 0), (2, 1)):
        wait("z", 0, dz, t)
        send(0, dz, t, "x+", "x-", "t")
    for dx, t in ((3, 1), (1, 0)):
        wait("x", dx, 0, t)
        send(dx, 0, t, "t")
    for dz in (3, 1, 2):
        for dx, t in ((3, 0), (1, 1)):
            wait("x", dx, dz, t)
            send(dx, dz, t, "x-" if t else "x+", "t")
        for dx, t in ((3, 1), (1, 0)):
            wait("x", dx, dz, t)
            send(dx, dz, t, "t")
    for dz in (0, 3, 1, 2):
        for t in (0, 1):
            wait("x", 2, dz, t)
            send(2, dz, t, "t")
    for dx in range(4):
        for dz in range(4):
            for t in (0, 1):
                wait("t", dx, dz, t)

    for c in sent:
        c.wait_send()
    for i, t, c in first:
        if i:
            c.wait_send()

    @pl.when(jnp.logical_not(me.late))
    def _():
        local_q.wait()
        for i in range(1, 8):
            q_copy(i, False)[1].wait_send()
        for i in range(1, 8):
            group = xor_bits(me.group, i)
            src = q_ref.at[:, cols(group, GROUP * HD)]
            copy(src, qg_ref.at[slot_of(group)], qs.at[i], qr.at[i], me.partner(group)).wait_recv()

    @pl.when(me.late)
    def _():
        for i in range(8):
            src, c = q_copy(i, True)
            if i == 0:

                @pl.when(own_sum)
                def _():
                    pltpu.make_async_copy(src, qg_ref.at[8], ls.at[2]).wait()

                @pl.when(jnp.logical_not(own_sum))
                def _():
                    c.wait_send()
            else:
                c.wait_send()

    @pl.when(jnp.logical_not(own_sum))
    def _():
        src = q_ref.at[:, cols(me.group, GROUP * HD)]
        copy(src, qg_ref.at[8], qs.at[0], qr.at[8], me.summary_owner()).wait_recv()


def collect_kernel(og_ref, out_ref, ss, rs, ls):
    me = Place()
    barrier = pltpu.get_barrier_semaphore()

    def greet(device):
        pl.semaphore_signal(barrier, inc=1, device_id=device, device_id_type=MESH)

    own_sum = me.own_summary()
    early = jnp.logical_not(me.late)

    @pl.when(early)
    def _():
        for i in range(1, 8):
            greet(me.partner(xor_bits(me.group, i)))

    @pl.when(me.late)
    def _():
        for i in range(1, 8):
            greet(me.summary_worker(xor_bits(me.group, i)))

        @pl.when(jnp.logical_not(own_sum))
        def _():
            greet(me.summary_worker(me.group))

    @pl.when(jnp.logical_not(own_sum))
    def _():
        pl.semaphore_wait(barrier, jnp.where(early, 8, 1))

    def copy(src, dst, send, recv, device):
        return pltpu.make_async_remote_copy(
            src_ref=src, dst_ref=dst, send_sem=send, recv_sem=recv, device_id=device, device_id_type=MESH
        )

    mine = out_ref.at[:, cols(me.group, GROUP * HD)]

    def own_copy(i):
        group = xor_bits(me.group, i)
        return copy(og_ref.at[slot_of(group)], mine, ss.at[i], rs.at[i], me.partner(group))

    summary_copy = copy(og_ref.at[8], mine, ss.at[8], rs.at[8 + me.group], me.summary_owner())
    local = pltpu.make_async_copy(og_ref.at[slot_of(me.group)], mine, ls.at[0])
    local_summary = pltpu.make_async_copy(og_ref.at[8], mine, ls.at[1])

    @pl.when(own_sum)
    def _():
        local_summary.start()

    @pl.when(jnp.logical_not(own_sum))
    def _():
        summary_copy.start()

    @pl.when(early)
    def _():
        for i in range(1, 8):
            own_copy(i).start()
        local.start()
        local.wait()
        for i in range(1, 8):
            group = xor_bits(me.group, i)
            dst = out_ref.at[:, cols(group, GROUP * HD)]
            copy(og_ref.at[slot_of(group)], dst, ss.at[i], rs.at[i], me.partner(group)).wait_recv()
        for i in range(1, 8):
            own_copy(i).wait_send()

    @pl.when(own_sum)
    def _():
        local_summary.wait()

    @pl.when(jnp.logical_not(own_sum))
    def _():
        summary_copy.wait_send()

    @pl.when(me.late)
    def _():
        for group in range(8):
            dst = out_ref.at[:, pl.ds(group * GROUP * HD, GROUP * HD)]
            c = copy(og_ref.at[8], dst, ss.at[8], rs.at[8 + group], me.partner(group))

            @pl.when(jnp.logical_not(jnp.logical_and(own_sum, me.group == group)))
            def _():
                c.wait_recv()


def attend_kernel(starts, q_hbm, kv_hbm, o_ref, qv, kv, qh, top, tot, acc, sems):
    me = Place()
    cq = pltpu.make_async_copy(q_hbm, qv, sems.at[0])
    cq.start()
    span = 1024
    loads = []
    for b in range(CTX // span):
        part = pl.ds(b * span, span)
        c = pltpu.make_async_copy(kv_hbm.at[:, part], kv.at[:, part], sems.at[1 + b])
        c.start()
        loads.append(c)
    cq.wait()
    rows = 4 * CHUNK
    for cl in range(2):
        for h in range(GROUP):
            for y in range(4):
                at = cl * GROUP * rows + h * rows + y * CHUNK
                qh[at : at + CHUNK] = qv[cl * 4 + y, :, h * HD : (h + 1) * HD]
    base = 2 * GROUP * rows
    for h in range(GROUP):
        qh[base + h * CHUNK : base + (h + 1) * CHUNK] = qv[8, :, h * HD : (h + 1) * HD]
    top[...] = jnp.full_like(top, NEG)
    tot[...] = jnp.zeros_like(tot)
    acc[...] = jnp.zeros_like(acc)
    for c in loads:
        c.wait()

    def tile(at, m, key_at, visible):
        part = pl.ds(at, m)
        keys = pl.ds(pl.multiple_of(key_at, HD), KEYS)
        s = lax.dot_general(
            qh[part], kv[0, keys], (((1,), (1,)), ((), ())), preferred_element_type=jnp.float32
        )
        if visible is not None:
            s = jnp.where(visible, s, NEG)
        old = top[part]
        new = jnp.maximum(old, jnp.max(s, axis=1, keepdims=True))
        top[part] = new
        w = jnp.exp2(s * RATE - jnp.concatenate([new * RATE] * (KEYS // 128), axis=1))
        factor = jnp.exp2((old - new) * RATE)
        lanes = w[:, :128]
        for j in range(1, KEYS // 128):
            lanes = lanes + w[:, j * 128 : (j + 1) * 128]
        tot[part] = tot[part] * factor + lanes
        acc[part] = acc[part] * factor + jnp.dot(
            w.astype(jnp.bfloat16), kv[1, keys], preferred_element_type=jnp.float32
        )

    def key_pos(m, key_at):
        return key_at + lax.broadcasted_iota(jnp.int32, (m, KEYS), 1)

    m = GROUP * CHUNK
    chunk = (me.zb * 2 + me.core) * 8 + me.x * 2 + me.zhi
    sum_pos = SUMMARY_AT + chunk * CHUNK + lax.broadcasted_iota(jnp.int32, (m, KEYS), 0) % CHUNK

    def summary_step(b, _):
        tile(base, m, b * KEYS, None)
        return 0

    lax.fori_loop(0, SUMMARY_AT // KEYS, summary_step, 0)
    for b in range(SUMMARY_AT // KEYS, CTX // KEYS):
        tile(base, m, b * KEYS, key_pos(m, b * KEYS) <= sum_pos)

    first_response = starts[1]

    @pl.when(jnp.logical_not(me.late))
    def _():
        for cl in range(2):
            p0 = (((me.x * 2 + me.zb) * 2 + cl) * 2 + me.core) * 256
            r = lax.broadcasted_iota(jnp.int32, (rows, 1), 0)
            pos = p0 + r // CHUNK * 64 + me.zhi * CHUNK + r % CHUNK
            own = jnp.zeros_like(pos)
            own_low = jnp.int32(0)
            own_high = jnp.int32(0)
            for j in range(10):
                own = jnp.where(starts[j] <= pos, starts[j], own)
                own_low = jnp.where(starts[j] <= p0, starts[j], own_low)
                own_high = jnp.where(starts[j] <= p0 + 255, starts[j], own_high)
            end = jnp.minimum(first_response, pos + 1)
            begin = jnp.maximum(first_response, own)
            here = cl * GROUP * rows

            def step(key_at, visible):
                for h in range(0, GROUP, 2):
                    both = None if visible is None else jnp.concatenate([visible, visible], axis=0)
                    tile(here + h * rows, 2 * rows, key_at, both)

            def prompt_step(b, _):
                key_at = b * KEYS
                clear = key_at + KEYS <= jnp.minimum(first_response, p0 + 1)

                @pl.when(clear)
                def _():
                    step(key_at, None)

                @pl.when(jnp.logical_not(clear))
                def _():
                    step(key_at, key_pos(rows, key_at) < end)

                return 0

            lax.fori_loop(0, (jnp.minimum(first_response, p0 + 256) + KEYS - 1) // KEYS, prompt_step, 0)
            low = jnp.maximum(own_low, first_response) // HD * HD
            high = jnp.maximum(own_high, first_response)

            def own_step(b, _):
                key_at = low + b * KEYS
                clear = jnp.logical_and(key_at >= high, key_at + KEYS <= p0 + 1)

                @pl.when(clear)
                def _():
                    step(key_at, None)

                @pl.when(jnp.logical_not(clear))
                def _():
                    k = key_pos(rows, key_at)
                    step(key_at, jnp.logical_and(k >= begin, k <= pos))

                return 0

            lax.fori_loop(0, (jnp.maximum(p0 + 256 - low, 0) + KEYS - 1) // KEYS, own_step, 0)

    def finish(at, m):
        part = pl.ds(at, m)
        return (acc[part] / jnp.sum(tot[part], axis=1, keepdims=True)).astype(o_ref.dtype)

    @pl.when(jnp.logical_not(me.late))
    def _():
        for cl in range(2):
            for h in range(GROUP):
                done = finish(cl * GROUP * rows + h * rows, rows)
                for y in range(4):
                    o_ref[cl * 4 + y, :, h * HD : (h + 1) * HD] = done[y * CHUNK : (y + 1) * CHUNK]

    for h in range(GROUP):
        o_ref[8, :, h * HD : (h + 1) * HD] = finish(base + h * CHUNK, CHUNK)


def per_device(query_states, key_states, value_states, seg_ids, seg_starts):
    anywhere = pl.BlockSpec(memory_space=pl.ANY)
    dma = pltpu.SemaphoreType.DMA
    qg, kv = pl.pallas_call(
        spread_kernel,
        out_shape=(
            jax.ShapeDtypeStruct((9, CHUNK, GROUP * HD), jnp.bfloat16),
            jax.ShapeDtypeStruct((2, 8, 2, 2, 4, 2, CHUNK, HD), jnp.bfloat16),
        ),
        in_specs=[anywhere] * 3,
        out_specs=(anywhere, anywhere),
        scratch_shapes=[dma((8,)), dma((9,)), dma((8, 2)), dma((8, 2)), dma((62,)), dma((62,)), dma((3,))],
        compiler_params=pltpu.CompilerParams(collective_id=0, has_side_effects=True),
        name="spread",
    )(query_states, key_states, value_states)
    lanes = 2 * GROUP * 4 * CHUNK + GROUP * CHUNK
    og = pl.pallas_call(
        attend_kernel,
        out_shape=jax.ShapeDtypeStruct((9, CHUNK, GROUP * HD), jnp.bfloat16),
        in_specs=[pl.BlockSpec(memory_space=pltpu.SMEM), anywhere, anywhere],
        out_specs=pl.BlockSpec(memory_space=pltpu.VMEM),
        scratch_shapes=[
            pltpu.VMEM((9, CHUNK, GROUP * HD), jnp.bfloat16),
            pltpu.VMEM((2, CTX, HD), jnp.bfloat16),
            pltpu.VMEM((lanes, HD), jnp.bfloat16),
            pltpu.VMEM((lanes, 128), jnp.float32),
            pltpu.VMEM((lanes, 128), jnp.float32),
            pltpu.VMEM((lanes, HD), jnp.float32),
            dma((9,)),
        ],
        compiler_params=pltpu.CompilerParams(vmem_limit_bytes=48 * 1024 * 1024),
        name="attend",
    )(seg_starts, qg, kv.reshape(2, CTX, HD))
    return pl.pallas_call(
        collect_kernel,
        out_shape=jax.ShapeDtypeStruct((CHUNK, 8 * GROUP * HD), jnp.bfloat16),
        in_specs=[anywhere],
        out_specs=anywhere,
        scratch_shapes=[dma((9,)), dma((16,)), dma((2,))],
        compiler_params=pltpu.CompilerParams(collective_id=1, has_side_effects=True),
        name="collect",
    )(og)


def solution(mesh):
    return jax.shard_map(
        per_device,
        mesh=mesh,
        in_specs=(
            P(("seq", "head"), None),
            P(("seq", "head"), None),
            P(("seq", "head"), None),
            P("seq"),
            P(),
        ),
        out_specs=P(("seq", "head"), None),
        check_vma=False,
    )
```
